32 devices in a mesh: rep: 2 (over x), rank: 16 (over z, y, core).
Axes of the slice: x: 2, y: 2, z: 4, core: 2. Of those that a mesh axis runs over, the one named last changes fastest.
Arguments:
- tokens: bfloat16 [4096, 2048], P(('rep', 'rank')), parts along dimension 0, may hold values from -6 to 6
- routes: int32 [4096, 8], P(('rep', 'rank')), parts along dimension 0, may hold values from 0 to 15, all different within a row; in each aligned block of 32 rows (0 to 31, 32 to 63, ...) at most 24 rows name the same one
- gate_weights: float32 [4096, 8], P(('rep', 'rank')), parts along dimension 0, may hold values from 0.05 to 0.5
- token_order: int32 [128, 32], P(('rep', 'rank')), parts along dimension 0, may hold values from 0 to 31, each once within a row
- w_gate: bfloat16 [16, 2048, 768], P('rank'), may hold values from -0.125 to 0.125
- w_up: bfloat16 [16, 2048, 768], P('rank'), may hold values from -0.125 to 0.125
- w_down: bfloat16 [16, 768, 2048], P('rank'), may hold values from -0.21875 to 0.21875
Outputs:
- mixed: bfloat16 [4096, 2048], P(('rep', 'rank')), parts along dimension 0
The draws below stay inside these ranges and needn't reach their ends.
There are 2 independent parts, one for each index of `rep`. The reference program is written for one: setup_inputs(seed, part) draws one part's arguments, and reference() takes and returns one part's arrays. A program takes and returns all parts, laid end to end along the dimension named above; an argument that names none is the same for every part. Nothing has to cross between parts.
Inputs may be any that keep to these rules, and one draw needn't show every extreme that they name: `routes`: each row names 8 different experts; every expert is named somewhere. In each aligned block of 32 rows no expert is named by more than 24 rows, and in every draw some block has an expert named by exactly 24 rows. `token_order`: each row is a permutation of the 32 row numbers of a block.
All inputs are finite; a program needn't handle non-finite values.
Results may differ from the reference program's by a relative error of at most 0.0058.
Values may be sent and summed in bfloat16 or wider, within the bound.
A program may use at most 128 MiB of HBM per device.

```python
import math
import jax
import jax.numpy as jnp
import numpy as np
from jax import lax

D = 2048
FF = 768
TOP = 8
BLOCKS = 4
BLOCK_ROWS = 32
EXPERTS = 16
TOKENS = 2048
CAP = 24
N_RANK = 16


def steps_of(key, extent, cuts, smallest, top_value):
    def one(position, blocks):
        steps = jax.random.uniform(jax.random.fold_in(jax.random.fold_in(key, 6), position), (blocks,), jnp.float32, smallest / len(cuts), top_value / len(cuts))
        return jnp.repeat(jnp.exp(steps), extent[position] // blocks).reshape((-1,) + (1,) * (len(extent) - position - 1))

    level = one(*cuts[0])
    for cut in cuts[1:]:
        level = level * one(*cut)
    return level


def routed_block(own_key, own, number, rows, count, top, limit, slope):
    sequence = jax.random.permutation(own_key, count)
    packed, ordinary = portions_of(count, rows * top, limit, slope, True), portions_of(count, rows * top, limit, slope, False)
    places = jnp.arange(count)

    def named(tallies, offset_by):
        used = int((tallies > 0).sum())
        fixed = max(1, used // 4)
        shifted = fixed + (places - fixed + offset_by * (used - fixed)) % max(1, count - fixed)
        return jnp.zeros((count,), jnp.int32).at[sequence[jnp.where(places < fixed, places, shifted)]].set(jnp.asarray(tallies, jnp.int32))

    tallies = jnp.where(number % 4 == 0, named(packed, number // 4), named(ordinary, number - number // 4 - 1))
    mixed = jax.random.permutation(jax.random.fold_in(own, 3), count)
    source_of, sink = mixed[0:count // 2 * 2:2], mixed[1:count // 2 * 2:2]
    margin = jnp.minimum(tallies[source_of] - 1, limit - tallies[sink]) // 2
    margin = jnp.where((source_of == sequence[0]) | (sink == sequence[0]) | (tallies[sink] == 0), 0, jnp.maximum(margin, 0))
    shifted = jax.random.randint(jax.random.fold_in(own, 4), (count // 2,), 0, 1 << 20) % (margin + 1)
    tallies = tallies.at[source_of].add(-shifted).at[sink].add(shifted)
    items = jnp.searchsorted(jnp.cumsum(tallies), jnp.arange(rows * top), side="right").astype(jnp.int32)
    listing = items.reshape(top, rows).T
    listing = listing[jax.random.permutation(jax.random.fold_in(own, 1), rows)]
    offset_by = jax.random.randint(jax.random.fold_in(own, 2), (rows, 1), 0, top)
    return jnp.take_along_axis(listing, (jnp.arange(top)[None, :] + offset_by) % top, axis=1)


def portions_of(amount, total, most, slope, full):
    weights = [(1 << 20) // math.isqrt(grade ** slope) + 1 for grade in range(1, amount + 1)]
    largest = most if full else min(most, max(-(-total // amount), total * weights[0] // sum(weights)))
    least = 1 if total - largest >= amount - 1 else 0
    holding, rest = [largest] + [least] * (amount - 1), total - largest - least * (amount - 1)
    while rest > 0:
        candidates = [i for i in range(1, amount) if holding[i] < largest] or [i for i in range(1, amount) if holding[i] < most]
        mass, remaining = sum([weights[i] for i in candidates]), rest
        for i in candidates:
            addition = min(most - holding[i], max(1, remaining * weights[i] // mass), rest)
            holding[i] = holding[i] + addition
            rest = rest - addition
    return np.array(holding)


def scatter_about(stream_key, extent, deviation, bound, cuts=(), kind=jnp.bfloat16):
    drawn = deviation * jax.random.normal(stream_key, extent, jnp.float32)
    if cuts:
        drawn = drawn * steps_of(stream_key, extent, cuts, -0.22, 0.18)
    return jnp.clip(drawn, -bound, bound).astype(kind)


def setup_inputs(seed: int = 0, part: int = 0) -> dict:
    key_of = jax.random.split(jax.random.key(seed), 8)
    part_splits = jax.random.split(jax.random.fold_in(key_of[7], part), 8)
    tokens = scatter_about(part_splits[0], (TOKENS, D), 1.0, 6.0, ((0, 16),))
    routes_keys = jax.random.split(jax.random.fold_in(part_splits[1], 1), TOKENS // BLOCK_ROWS)
    routes_turns = jax.random.permutation(jax.random.fold_in(part_splits[1], 3), TOKENS // BLOCK_ROWS)
    routes = jax.vmap(lambda own, number: routed_block(jax.random.fold_in(part_splits[1], 2), own, number, BLOCK_ROWS, EXPERTS, TOP, CAP, 2))(routes_keys, routes_turns).reshape((TOKENS, TOP))
    gate_weights = jnp.clip(jnp.exp(math.log(0.5) - 2.3025851 * jax.random.uniform(part_splits[2], (TOKENS, TOP), jnp.float32) ** steps_of(part_splits[2], (TOKENS, TOP), ((0, 16),), -0.2, 0.2)), 0.05, 0.5)
    token_order = jax.vmap(lambda own: jax.random.permutation(own, BLOCK_ROWS))(jax.random.split(part_splits[3], (N_RANK * BLOCKS))).reshape((N_RANK * BLOCKS, BLOCK_ROWS)).astype(jnp.int32)
    w_gate = scatter_about(key_of[4], (EXPERTS, D, FF), D ** -0.5, 0.125, ((0, 16),))
    w_up = scatter_about(key_of[5], (EXPERTS, D, FF), D ** -0.5, 0.125, ((0, 16),))
    w_down = scatter_about(key_of[6], (EXPERTS, FF, D), FF ** -0.5, 0.21875, ((0, 16),))
    return dict(tokens=tokens, routes=routes, gate_weights=gate_weights, token_order=token_order, w_gate=w_gate, w_up=w_up, w_down=w_down)


def reference(tokens, routes, gate_weights, token_order, w_gate, w_up, w_down):
    row_bound = N_RANK * BLOCKS * CAP

    def add_expert(running, expert):
        chosen = routes == expert
        weight_sum = jnp.sum(jnp.where(chosen, gate_weights, 0.0), axis=1)
        present = jnp.any(chosen, axis=1)
        picked = jnp.nonzero(present, size=row_bound, fill_value=0)[0].astype(jnp.int32)
        filled = jnp.arange(row_bound, dtype=jnp.int32) < jnp.sum(present.astype(jnp.int32))
        picked_rows = tokens[picked]
        gate_mat = lax.dynamic_index_in_dim(w_gate, expert, 0, keepdims=False)
        up_mat = lax.dynamic_index_in_dim(w_up, expert, 0, keepdims=False)
        down_mat = lax.dynamic_index_in_dim(w_down, expert, 0, keepdims=False)
        gate_proj = jnp.dot(picked_rows, gate_mat, preferred_element_type=jnp.float32)
        up_proj = jnp.dot(picked_rows, up_mat, preferred_element_type=jnp.float32)
        hidden = (jax.nn.silu(gate_proj) * up_proj).astype(jnp.bfloat16)
        expert_out = jnp.dot(hidden, down_mat, preferred_element_type=jnp.float32).astype(jnp.bfloat16)
        factor = jnp.where(filled, weight_sum[picked], 0.0)
        running = running.at[picked].add(factor[:, None] * expert_out.astype(jnp.float32))
        return running, None

    start = jnp.zeros((TOKENS, D), jnp.float32)
    combined, _ = lax.scan(add_expert, start, jnp.arange(EXPERTS, dtype=jnp.int32))
    rounded = combined.astype(jnp.bfloat16).reshape(N_RANK * BLOCKS, BLOCK_ROWS, D)
    mixed = jnp.take_along_axis(rounded, token_order[:, :, None], axis=1)
    return mixed.reshape(TOKENS, D)
```

```python
import jax
import jax.numpy as jnp
from jax import lax
from jax.sharding import PartitionSpec as P


def per_device(tokens, routes, gate_weights, token_order, w_gate, w_up, w_down):
    rank = lax.axis_index("rank")
    rows, features = tokens.shape
    blocks, block_rows = token_order.shape

    everyone = lax.all_gather(tokens, "rank", axis=0, tiled=True)
    all_routes = lax.all_gather(routes, "rank", axis=0, tiled=True)
    all_gates = lax.all_gather(gate_weights, "rank", axis=0, tiled=True)
    factor = jnp.sum(jnp.where(all_routes == rank, all_gates, 0.0), axis=1)

    gate_proj = jnp.dot(everyone, w_gate[0], preferred_element_type=jnp.float32)
    up_proj = jnp.dot(everyone, w_up[0], preferred_element_type=jnp.float32)
    hidden = (jax.nn.silu(gate_proj) * up_proj).astype(jnp.bfloat16)
    expert_out = jnp.dot(hidden, w_down[0], preferred_element_type=jnp.float32)
    weighed = (factor[:, None] * expert_out).astype(jnp.bfloat16)
    combined = lax.psum_scatter(weighed, "rank", scatter_dimension=0, tiled=True)

    order = token_order + jnp.arange(blocks, dtype=jnp.int32)[:, None] * block_rows
    pick = (order.reshape(-1)[:, None] == jnp.arange(rows, dtype=jnp.int32)[None, :])
    return jnp.dot(
        pick.astype(jnp.bfloat16), combined, preferred_element_type=jnp.float32
    ).astype(jnp.bfloat16)


def solution(mesh):
    return jax.shard_map(
        per_device,
        mesh=mesh,
        in_specs=(
            P(("rep", "rank"), None),
            P(("rep", "rank"), None),
            P(("rep", "rank"), None),
            P(("rep", "rank"), None),
            P("rank", None, None),
            P("rank", None, None),
            P("rank", None, None),
        ),
        out_specs=P(("rep", "rank"), None),
        check_vma=False,
    )
```

```python
import functools

import jax
import jax.numpy as jnp
from jax import lax
from jax.experimental import pallas as pl
from jax.experimental.pallas import tpu as pltpu
from jax.sharding import PartitionSpec as P

MESH = pl.DeviceIdType.MESH


def kernel(
    n, tokens, table, w_gate, w_up, w_down, out,
    held, factors, part, from_core, from_y, from_z, gate_v, up_v, down_v, hidden,
    own_sem, w_sem, f_send, f_recv, ag_send, ag_recv,
    core_send, core_recv, y_send, y_recv, z_send, z_recv, out_sem,
):
    depth = n // 4
    rows, features = tokens.shape
    width = gate_v.shape[1]
    me = lax.axis_index("rank")
    z, y, c = me // 4, (me // 2) % 2, me % 2
    sibling = me + 1 - 2 * c
    across = me + 2 - 4 * y

    own = pltpu.make_async_copy(tokens, held.at[me], own_sem)
    own.start()
    loads = [
        pltpu.make_async_copy(a, b, w_sem.at[i])
        for i, (a, b) in enumerate(((w_gate, gate_v), (w_up, up_v), (w_down, down_v)))
    ]
    for load in loads:
        load.start()

    barrier = pltpu.get_barrier_semaphore()

    @pl.loop(1, n)
    def _(i):
        pl.semaphore_signal(barrier, inc=1, device_id={"rank": (me + i) % n}, device_id_type=MESH)

    pl.semaphore_wait(barrier, n - 1)

    def order(k):
        near = jnp.minimum(z, depth - 1 - z)
        step = (k + 1) // 2
        both = jnp.where(k % 2 == 1, z + step, z - step)
        one = jnp.where(z <= depth - 1 - z, k, depth - 1 - k)
        return jnp.where(k <= 2 * near, both, one)

    def remote(source, target, send, recv, to):
        return pltpu.make_async_remote_copy(
            src_ref=source, dst_ref=target, send_sem=send, recv_sem=recv,
            device_id={"rank": to}, device_id_type=MESH,
        )

    def shard(b, way, to):
        return remote(held.at[b], held.at[b], ag_send.at[way, b], ag_recv.at[b], to)

    def weight(to, source):
        return remote(table.at[to], factors.at[source], f_send.at[to], f_recv.at[source], to)

    def half(pair, side):
        b = 2 * pair + side
        return remote(part.at[b], from_core.at[pair], core_send.at[pair], core_recv.at[pair], sibling)

    def cross(zo):
        return remote(
            part.at[zo * 4 + (1 - y) * 2 + c], from_y.at[zo], y_send.at[zo], y_recv.at[zo], across
        )

    def along(zo, way, to):
        return remote(
            part.at[zo * 4 + y * 2 + c], from_z.at[way, zo], z_send.at[zo], z_recv.at[way, zo], to
        )

    def forward(k):
        zo = order(k)
        b = zo * 4 + y * 2 + c

        @pl.when(zo != z)
        def _():
            shard(b, 0, me).wait_recv()

        @pl.when((zo <= z) & (z < depth - 1))
        def _():
            shard(b, 0, me + 4).start()

        @pl.when((zo >= z) & (z > 0))
        def _():
            shard(b, 1, me - 4).start()

        shard(b, 2, across).start()
        shard(b, 3, sibling).start()

    def expert(pair):
        x = held[pl.ds(2 * pair, 2)].reshape(2 * rows, features)

        @pl.loop(0, width // 256)
        def _(i):
            cols = pl.ds(pl.multiple_of(i * 256, 256), 256)
            g = jnp.dot(x, gate_v[:, cols], preferred_element_type=jnp.float32)
            u = jnp.dot(x, up_v[:, cols], preferred_element_type=jnp.float32)
            hidden[:, cols] = (g / (1.0 + jnp.exp(-g)) * u).astype(jnp.bfloat16)

        eye = lax.broadcasted_iota(jnp.int32, (rows, rows), 0) == lax.broadcasted_iota(
            jnp.int32, (rows, rows), 1
        )
        scale = jnp.concatenate(
            [
                jnp.sum(jnp.where(eye, factors[2 * pair + s][0:1, :], 0.0), axis=1, keepdims=True)
                for s in range(2)
            ],
            axis=0,
        )

        @pl.loop(0, features // 512)
        def _(i):
            cols = pl.ds(pl.multiple_of(i * 512, 512), 512)
            o = jnp.dot(hidden[...], down_v[:, cols], preferred_element_type=jnp.float32)
            o = (o * scale).astype(jnp.bfloat16)
            part[pl.ds(2 * pair, 2), :, cols] = o.reshape(2, rows, 512)

    def add(b, terms):
        @pl.loop(0, rows // 16)
        def _(i):
            r = pl.ds(pl.multiple_of(i * 16, 16), 16)
            total = part[b, r, :].astype(jnp.float32)
            for term in terms:
                total += term[r, :].astype(jnp.float32)
            part[b, r, :] = total.astype(jnp.bfloat16)

    def reduce_pairs(k):
        zo = order(k)
        for yo in (1 - y, y):
            pair = 2 * zo + yo
            half(pair, c).wait_recv()
            add(2 * pair + c, [from_core.at[pair]])
            if yo is not y:
                cross(zo).start()

    @pl.loop(1, n)
    def _(i):
        weight((me + i) % n, me).start()

    mine = pltpu.make_async_copy(table.at[me], factors.at[me], f_send.at[me])
    mine.start()
    own.wait()
    forward(0)
    mine.wait()
    for load in loads:
        load.wait()

    @pl.loop(1, n)
    def _(i):
        weight(me, (me + i) % n).wait_recv()

    @pl.loop(0, depth)
    def _(k):
        zo = order(k)
        shard(zo * 4 + y * 2 + 1 - c, 3, sibling).wait_recv()
        expert(2 * zo + y)
        half(2 * zo + y, 1 - c).start()

        @pl.when(k < depth - 1)
        def _():
            forward(k + 1)

        @pl.when(k > 0)
        def _():
            reduce_pairs(k - 1)

        b = zo * 4 + (1 - y) * 2 + c
        shard(b, 2, across).wait_recv()
        shard(b, 3, sibling).start()
        shard(b + 1 - 2 * c, 3, sibling).wait_recv()
        expert(2 * zo + 1 - y)
        half(2 * zo + 1 - y, 1 - c).start()

    reduce_pairs(depth - 1)

    @pl.loop(0, depth)
    def _(i):
        zo = order(depth - 1 - i)
        b = zo * 4 + y * 2 + c
        cross(zo).wait_recv()
        add(b, [from_y.at[zo]])

        @pl.when((zo >= z) & (z > 0))
        def _():
            along(zo, 0, me).wait_recv()
            add(b, [from_z.at[0, zo]])

        @pl.when((zo <= z) & (z < depth - 1))
        def _():
            along(zo, 1, me).wait_recv()
            add(b, [from_z.at[1, zo]])

        @pl.when(zo > z)
        def _():
            along(zo, 0, me + 4).start()

        @pl.when(zo < z)
        def _():
            along(zo, 1, me - 4).start()

    done = pltpu.make_async_copy(part.at[me], out, out_sem)
    done.start()

    @pl.loop(1, n)
    def _(i):
        weight((me + i) % n, me).wait_send()

    @pl.loop(0, depth)
    def _(zo):
        b = zo * 4 + y * 2 + c

        @pl.when((zo <= z) & (z < depth - 1))
        def _():
            shard(b, 0, me + 4).wait_send()

        @pl.when((zo >= z) & (z > 0))
        def _():
            shard(b, 1, me - 4).wait_send()

        shard(b, 2, across).wait_send()
        shard(b, 3, sibling).wait_send()
        shard(zo * 4 + (1 - y) * 2 + c, 3, sibling).wait_send()
        half(2 * zo, 1 - c).wait_send()
        half(2 * zo + 1, 1 - c).wait_send()
        cross(zo).wait_send()

        @pl.when(zo > z)
        def _():
            along(zo, 0, me + 4).wait_send()

        @pl.when(zo < z)
        def _():
            along(zo, 1, me - 4).wait_send()

    done.wait()


def exchange(n, tokens, table, w_gate, w_up, w_down):
    rows, features = tokens.shape
    width = w_gate.shape[1]
    depth = n // 4
    bf, dma = jnp.bfloat16, pltpu.SemaphoreType.DMA
    return pl.pallas_call(
        functools.partial(kernel, n),
        out_shape=jax.ShapeDtypeStruct((rows, features), bf),
        in_specs=[
            pl.BlockSpec(memory_space=pl.ANY),
            pl.BlockSpec(memory_space=pltpu.VMEM),
            pl.BlockSpec(memory_space=pl.ANY),
            pl.BlockSpec(memory_space=pl.ANY),
            pl.BlockSpec(memory_space=pl.ANY),
        ],
        out_specs=pl.BlockSpec(memory_space=pl.ANY),
        scratch_shapes=[
            pltpu.VMEM((n, rows, features), bf),
            pltpu.VMEM((n, 8, rows), jnp.float32),
            pltpu.VMEM((n, rows, features), bf),
            pltpu.VMEM((n // 2, rows, features), bf),
            pltpu.VMEM((depth, rows, features), bf),
            pltpu.VMEM((2, depth, rows, features), bf),
            pltpu.VMEM((features, width), bf),
            pltpu.VMEM((features, width), bf),
            pltpu.VMEM((width, features), bf),
            pltpu.VMEM((2 * rows, width), bf),
            dma, dma((3,)), dma((n,)), dma((n,)), dma((4, n)), dma((n,)),
            dma((n // 2,)), dma((n // 2,)), dma((depth,)), dma((depth,)),
            dma((depth,)), dma((2, depth)), dma,
        ],
        compiler_params=pltpu.CompilerParams(
            collective_id=0, has_side_effects=True, vmem_limit_bytes=56 * 1024 * 1024
        ),
        cost_estimate=pl.CostEstimate(
            flops=6 * n * rows * features * width,
            bytes_accessed=6 * features * width + 4 * rows * features,
            transcendentals=n * rows * width,
        ),
    )(tokens, table, w_gate, w_up, w_down)


def collectives(tokens, routes, gate_weights, w_gate, w_up, w_down):
    rank = lax.axis_index("rank")
    everyone = lax.all_gather(tokens, "rank", axis=0, tiled=True)
    all_routes = lax.all_gather(routes, "rank", axis=0, tiled=True)
    all_gates = lax.all_gather(gate_weights, "rank", axis=0, tiled=True)
    factor = jnp.sum(jnp.where(all_routes == rank, all_gates, 0.0), axis=1)
    gate_proj = jnp.dot(everyone, w_gate, preferred_element_type=jnp.float32)
    up_proj = jnp.dot(everyone, w_up, preferred_element_type=jnp.float32)
    hidden = (jax.nn.silu(gate_proj) * up_proj).astype(jnp.bfloat16)
    expert_out = jnp.dot(hidden, w_down, preferred_element_type=jnp.float32)
    weighed = (factor[:, None] * expert_out).astype(jnp.bfloat16)
    return lax.psum_scatter(weighed, "rank", scatter_dimension=0, tiled=True)


def per_device(tokens, routes, gate_weights, token_order, w_gate, w_up, w_down):
    n = lax.axis_size("rank")
    rows, features = tokens.shape
    blocks, block_rows = token_order.shape
    own_weights = (w_gate[0], w_up[0], w_down[0])

    if n % 4 == 0 and n * rows * features <= 4 * 1024 * 1024:
        chosen = routes.T[None] == jnp.arange(n, dtype=jnp.int32)[:, None, None]
        table = jnp.sum(jnp.where(chosen, gate_weights.T[None], 0.0), axis=1)
        table = jnp.broadcast_to(table[:, None, :], (n, 8, rows))
        combined = exchange(n, tokens, table, *own_weights)
    else:
        combined = collectives(tokens, routes, gate_weights, *own_weights)

    order = token_order + jnp.arange(blocks, dtype=jnp.int32)[:, None] * block_rows
    pick = (order.reshape(-1)[:, None] == jnp.arange(rows, dtype=jnp.int32)[None, :])
    return jnp.dot(
        pick.astype(jnp.bfloat16), combined, preferred_element_type=jnp.float32
    ).astype(jnp.bfloat16)


def solution(mesh):
    return jax.shard_map(
        per_device,
        mesh=mesh,
        in_specs=(
            P(("rep", "rank"), None),
            P(("rep", "rank"), None),
            P(("rep", "rank"), None),
            P(("rep", "rank"), None),
            P("rank", None, None),
            P("rank", None, None),
            P("rank", None, None),
        ),
        out_specs=P(("rep", "rank"), None),
        check_vma=False,
    )
```

```python
import functools

import jax
import jax.numpy as jnp
from jax import lax
from jax.experimental import pallas as pl
from jax.experimental.pallas import tpu as pltpu
from jax.sharding import PartitionSpec as P

MESH = pl.DeviceIdType.MESH
CHUNKS = 2


def kernel(
    n, tokens, table, w_gate, w_up, w_down, out,
    held, factors, part, from_core, from_y, from_z, gate_v, up_v, down_v, hidden,
    own_sem, w_sem, f_send, f_recv, ag_send, ag_recv,
    core_send, core_recv, y_send, y_recv, z_send, z_recv, out_sem,
):
    depth = n // 4
    rows, features = tokens.shape
    width = gate_v.shape[1]
    me = lax.axis_index("rank")
    z, y, c = me // 4, (me // 2) % 2, me % 2
    sibling = me + 1 - 2 * c
    across = me + 2 - 4 * y

    own = pltpu.make_async_copy(tokens, held.at[me], own_sem)
    own.start()
    loads = [
        pltpu.make_async_copy(a, b, w_sem.at[i])
        for i, (a, b) in enumerate(((w_gate, gate_v), (w_up, up_v), (w_down, down_v)))
    ]
    for load in loads:
        load.start()

    barrier = pltpu.get_barrier_semaphore()

    @pl.loop(1, n)
    def _(i):
        pl.semaphore_signal(barrier, inc=1, device_id={"rank": (me + i) % n}, device_id_type=MESH)

    pl.semaphore_wait(barrier, n - 1)

    def order(k):
        near = jnp.minimum(z, depth - 1 - z)
        step = (k + 1) // 2
        low = z <= depth - 1 - z
        both = jnp.where((k % 2 == 1) == low, z + step, z - step)
        one = jnp.where(low, k, depth - 1 - k)
        return jnp.where(k <= 2 * near, both, one)

    def remote(source, target, send, recv, to):
        return pltpu.make_async_remote_copy(
            src_ref=source, dst_ref=target, send_sem=send, recv_sem=recv,
            device_id={"rank": to}, device_id_type=MESH,
        )

    def shard(b, way, to):
        return remote(held.at[b], held.at[b], ag_send.at[way, b], ag_recv.at[b], to)

    def weight(to, source):
        return remote(table.at[to], factors.at[source], f_send.at[to], f_recv.at[source], to)

    def half(pair, side):
        b = 2 * pair + side
        return remote(part.at[b], from_core.at[pair], core_send.at[pair], core_recv.at[pair], sibling)

    def chunk(h):
        return pl.ds(h * (rows // CHUNKS), rows // CHUNKS)

    def cross(zo, h):
        return remote(
            part.at[zo * 4 + (1 - y) * 2 + c, chunk(h)], from_y.at[zo, chunk(h)],
            y_send.at[zo, h], y_recv.at[zo, h], across,
        )

    def along(zo, way, h, to):
        return remote(
            part.at[zo * 4 + y * 2 + c, chunk(h)], from_z.at[way, zo, chunk(h)],
            z_send.at[zo, h], z_recv.at[way, zo, h], to,
        )

    def forward(k):
        zo = order(k)
        b = zo * 4 + y * 2 + c

        @pl.when(zo != z)
        def _():
            shard(b, 0, me).wait_recv()

        @pl.when((zo <= z) & (z < depth - 1))
        def _():
            shard(b, 0, me + 4).start()

        @pl.when((zo >= z) & (z > 0))
        def _():
            shard(b, 1, me - 4).start()

        shard(b, 2, across).start()
        shard(b, 3, sibling).start()

    def expert(pair):
        x = held[pl.ds(2 * pair, 2)].reshape(2 * rows, features)

        @pl.loop(0, width // 256)
        def _(i):
            cols = pl.ds(pl.multiple_of(i * 256, 256), 256)
            g = jnp.dot(x, gate_v[:, cols], preferred_element_type=jnp.float32)
            u = jnp.dot(x, up_v[:, cols], preferred_element_type=jnp.float32)
            hidden[:, cols] = (g / (1.0 + jnp.exp(-g)) * u).astype(jnp.bfloat16)

        eye = lax.broadcasted_iota(jnp.int32, (rows, rows), 0) == lax.broadcasted_iota(
            jnp.int32, (rows, rows), 1
        )
        scale = jnp.concatenate(
            [
                jnp.sum(jnp.where(eye, factors[2 * pair + s][0:1, :], 0.0), axis=1, keepdims=True)
                for s in range(2)
            ],
            axis=0,
        )

        @pl.loop(0, features // 512)
        def _(i):
            cols = pl.ds(pl.multiple_of(i * 512, 512), 512)
            o = jnp.dot(hidden[...], down_v[:, cols], preferred_element_type=jnp.float32)
            o = (o * scale).astype(jnp.bfloat16)
            part[pl.ds(2 * pair, 2), :, cols] = o.reshape(2, rows, 512)

    def add(b, term, h):
        size = rows // CHUNKS

        @pl.loop(0, size // 16)
        def _(i):
            r = pl.ds(pl.multiple_of(h * size + i * 16, 16), 16)
            total = part[b, r, :].astype(jnp.float32) + term[r, :].astype(jnp.float32)
            part[b, r, :] = total.astype(jnp.bfloat16)

    def reduce_pairs(k):
        zo = order(k)
        for yo in (1 - y, y):
            pair = 2 * zo + yo
            half(pair, c).wait_recv()
            for h in range(CHUNKS):
                add(2 * pair + c, from_core.at[pair], h)
                if yo is not y:
                    cross(zo, h).start()

    @pl.loop(1, n)
    def _(i):
        weight((me + i) % n, me).start()

    mine = pltpu.make_async_copy(table.at[me], factors.at[me], f_send.at[me])
    mine.start()
    own.wait()
    forward(0)
    mine.wait()
    for load in loads:
        load.wait()

    @pl.loop(1, n)
    def _(i):
        weight(me, (me + i) % n).wait_recv()

    @pl.loop(0, depth)
    def _(k):
        zo = order(k)
        shard(zo * 4 + y * 2 + 1 - c, 3, sibling).wait_recv()
        expert(2 * zo + y)
        half(2 * zo + y, 1 - c).start()

        @pl.when(k < depth - 1)
        def _():
            forward(k + 1)

        if depth > 3:

            @pl.when(k == depth - 1)
            def _():
                reduce_pairs(1)

        b = zo * 4 + (1 - y) * 2 + c
        shard(b, 2, across).wait_recv()
        shard(b, 3, sibling).start()
        shard(b + 1 - 2 * c, 3, sibling).wait_recv()
        expert(2 * zo + 1 - y)
        half(2 * zo + 1 - y, 1 - c).start()

    last = [k for k in reversed(range(depth)) if depth < 4 or k != 1]

    @pl.loop(0, len(last))
    def _(i):
        reduce_pairs(jnp.where(i == len(last) - 1, 0, depth - 1 - i))

    @pl.loop(0, depth)
    def _(i):
        ends = jnp.where(i == depth - 1, 0, jnp.where(i == 0, 1, depth - i))
        zo = order(jnp.where((z == 0) | (z == depth - 1), ends, depth - 1 - i))
        b = zo * 4 + y * 2 + c

        @pl.loop(0, CHUNKS)
        def _(h):
            cross(zo, h).wait_recv()
            add(b, from_y.at[zo], h)

            @pl.when((zo >= z) & (z > 0))
            def _():
                along(zo, 0, h, me).wait_recv()
                add(b, from_z.at[0, zo], h)

            @pl.when((zo <= z) & (z < depth - 1))
            def _():
                along(zo, 1, h, me).wait_recv()
                add(b, from_z.at[1, zo], h)

            @pl.when(zo > z)
            def _():
                along(zo, 0, h, me + 4).start()

            @pl.when(zo < z)
            def _():
                along(zo, 1, h, me - 4).start()

    done = pltpu.make_async_copy(part.at[me], out, out_sem)
    done.start()

    @pl.loop(1, n)
    def _(i):
        weight((me + i) % n, me).wait_send()

    @pl.loop(0, depth)
    def _(zo):
        b = zo * 4 + y * 2 + c

        @pl.when((zo <= z) & (z < depth - 1))
        def _():
            shard(b, 0, me + 4).wait_send()

        @pl.when((zo >= z) & (z > 0))
        def _():
            shard(b, 1, me - 4).wait_send()

        shard(b, 2, across).wait_send()
        shard(b, 3, sibling).wait_send()
        shard(zo * 4 + (1 - y) * 2 + c, 3, sibling).wait_send()
        half(2 * zo, 1 - c).wait_send()
        half(2 * zo + 1, 1 - c).wait_send()
        for h in range(CHUNKS):
            cross(zo, h).wait_send()

        @pl.when(zo > z)
        def _():
            for h in range(CHUNKS):
                along(zo, 0, h, me + 4).wait_send()

        @pl.when(zo < z)
        def _():
            for h in range(CHUNKS):
                along(zo, 1, h, me - 4).wait_send()

    done.wait()


def exchange(n, tokens, table, w_gate, w_up, w_down):
    rows, features = tokens.shape
    width = w_gate.shape[1]
    depth = n // 4
    bf, dma = jnp.bfloat16, pltpu.SemaphoreType.DMA
    return pl.pallas_call(
        functools.partial(kernel, n),
        out_shape=jax.ShapeDtypeStruct((rows, features), bf),
        in_specs=[
            pl.BlockSpec(memory_space=pl.ANY),
            pl.BlockSpec(memory_space=pltpu.VMEM),
            pl.BlockSpec(memory_space=pl.ANY),
            pl.BlockSpec(memory_space=pl.ANY),
            pl.BlockSpec(memory_space=pl.ANY),
        ],
        out_specs=pl.BlockSpec(memory_space=pl.ANY),
        scratch_shapes=[
            pltpu.VMEM((n, rows, features), bf),
            pltpu.VMEM((n, 8, rows), jnp.float32),
            pltpu.VMEM((n, rows, features), bf),
            pltpu.VMEM((n // 2, rows, features), bf),
            pltpu.VMEM((depth, rows, features), bf),
            pltpu.VMEM((2, depth, rows, features), bf),
            pltpu.VMEM((features, width), bf),
            pltpu.VMEM((features, width), bf),
            pltpu.VMEM((width, features), bf),
            pltpu.VMEM((2 * rows, width), bf),
            dma, dma((3,)), dma((n,)), dma((n,)), dma((4, n)), dma((n,)),
            dma((n // 2,)), dma((n // 2,)), dma((depth, CHUNKS)), dma((depth, CHUNKS)),
            dma((depth, CHUNKS)), dma((2, depth, CHUNKS)), dma,
        ],
        compiler_params=pltpu.CompilerParams(
            collective_id=0, has_side_effects=True, vmem_limit_bytes=56 * 1024 * 1024
        ),
        cost_estimate=pl.CostEstimate(
            flops=6 * n * rows * features * width,
            bytes_accessed=6 * features * width + 4 * rows * features,
            transcendentals=n * rows * width,
        ),
    )(tokens, table, w_gate, w_up, w_down)


def collectives(tokens, routes, gate_weights, w_gate, w_up, w_down):
    rank = lax.axis_index("rank")
    everyone = lax.all_gather(tokens, "rank", axis=0, tiled=True)
    all_routes = lax.all_gather(routes, "rank", axis=0, tiled=True)
    all_gates = lax.all_gather(gate_weights, "rank", axis=0, tiled=True)
    factor = jnp.sum(jnp.where(all_routes == rank, all_gates, 0.0), axis=1)
    gate_proj = jnp.dot(everyone, w_gate, preferred_element_type=jnp.float32)
    up_proj = jnp.dot(everyone, w_up, preferred_element_type=jnp.float32)
    hidden = (jax.nn.silu(gate_proj) * up_proj).astype(jnp.bfloat16)
    expert_out = jnp.dot(hidden, w_down, preferred_element_type=jnp.float32)
    weighed = (factor[:, None] * expert_out).astype(jnp.bfloat16)
    return lax.psum_scatter(weighed, "rank", scatter_dimension=0, tiled=True)


def per_device(tokens, routes, gate_weights, token_order, w_gate, w_up, w_down):
    n = lax.axis_size("rank")
    rows, features = tokens.shape
    blocks, block_rows = token_order.shape
    own_weights = (w_gate[0], w_up[0], w_down[0])

    if n % 4 == 0 and n <= 16 and n * rows * features <= 4 * 1024 * 1024:
        chosen = routes.T[None] == jnp.arange(n, dtype=jnp.int32)[:, None, None]
        table = jnp.sum(jnp.where(chosen, gate_weights.T[None], 0.0), axis=1)
        table = jnp.broadcast_to(table[:, None, :], (n, 8, rows))
        combined = exchange(n, tokens, table, *own_weights)
    else:
        combined = collectives(tokens, routes, gate_weights, *own_weights)

    order = token_order + jnp.arange(blocks, dtype=jnp.int32)[:, None] * block_rows
    pick = (order.reshape(-1)[:, None] == jnp.arange(rows, dtype=jnp.int32)[None, :])
    return jnp.dot(
        pick.astype(jnp.bfloat16), combined, preferred_element_type=jnp.float32
    ).astype(jnp.bfloat16)


def solution(mesh):
    return jax.shard_map(
        per_device,
        mesh=mesh,
        in_specs=(
            P(("rep", "rank"), None),
            P(("rep", "rank"), None),
            P(("rep", "rank"), None),
            P(("rep", "rank"), None),
            P("rank", None, None),
            P("rank", None, None),
            P("rank", None, None),
        ),
        out_specs=P(("rep", "rank"), None),
        check_vma=False,
    )
```

```python
import functools

import jax
import jax.numpy as jnp
from jax import lax
from jax.experimental import pallas as pl
from jax.experimental.pallas import tpu as pltpu
from jax.sharding import PartitionSpec as P

MESH = pl.DeviceIdType.MESH
CHUNKS = 4


def kernel(
    n, tokens, table, w_gate, w_up, w_down, out,
    held, factors, part, from_core, from_y, from_z, gate_v, up_v, down_v, hidden,
    own_sem, w_sem, f_send, f_recv, ag_send, ag_recv,
    core_send, core_recv, y_send, y_recv, z_send, z_recv, out_sem,
):
    depth = n // 4
    rows, features = tokens.shape
    width = gate_v.shape[1]
    me = lax.axis_index("rank")
    z, y, c = me // 4, (me // 2) % 2, me % 2
    sibling = me + 1 - 2 * c
    across = me + 2 - 4 * y

    own = pltpu.make_async_copy(tokens, held.at[me], own_sem)
    own.start()
    loads = [
        pltpu.make_async_copy(a, b, w_sem.at[i])
        for i, (a, b) in enumerate(((w_gate, gate_v), (w_up, up_v), (w_down, down_v)))
    ]
    for load in loads:
        load.start()

    barrier = pltpu.get_barrier_semaphore()

    @pl.loop(1, n)
    def _(i):
        pl.semaphore_signal(barrier, inc=1, device_id={"rank": (me + i) % n}, device_id_type=MESH)

    pl.semaphore_wait(barrier, n - 1)

    def order(k):
        near = jnp.minimum(z, depth - 1 - z)
        step = (k + 1) // 2
        low = z <= depth - 1 - z
        both = jnp.where((k % 2 == 1) == low, z + step, z - step)
        one = jnp.where(low, k, depth - 1 - k)
        return jnp.where(k <= 2 * near, both, one)

    def remote(source, target, send, recv, to):
        return pltpu.make_async_remote_copy(
            src_ref=source, dst_ref=target, send_sem=send, recv_sem=recv,
            device_id={"rank": to}, device_id_type=MESH,
        )

    def shard(b, way, to):
        return remote(held.at[b], held.at[b], ag_send.at[way, b], ag_recv.at[b], to)

    def weight(to, source):
        return remote(table.at[to], factors.at[source], f_send.at[to], f_recv.at[source], to)

    def half(pair, side):
        b = 2 * pair + side
        return remote(part.at[b], from_core.at[pair], core_send.at[pair], core_recv.at[pair], sibling)

    def chunk(h):
        return pl.ds(h * (rows // CHUNKS), rows // CHUNKS)

    def cross(zo, h):
        return remote(
            part.at[zo * 4 + (1 - y) * 2 + c, chunk(h)], from_y.at[zo, chunk(h)],
            y_send.at[zo, h], y_recv.at[zo, h], across,
        )

    def along(zo, way, h, to):
        return remote(
            part.at[zo * 4 + y * 2 + c, chunk(h)], from_z.at[way, zo, chunk(h)],
            z_send.at[zo, h], z_recv.at[way, zo, h], to,
        )

    def forward(k):
        zo = order(k)
        b = zo * 4 + y * 2 + c

        @pl.when(zo != z)
        def _():
            shard(b, 0, me).wait_recv()

        @pl.when((zo <= z) & (z < depth - 1))
        def _():
            shard(b, 0, me + 4).start()

        @pl.when((zo >= z) & (z > 0))
        def _():
            shard(b, 1, me - 4).start()

        shard(b, 2, across).start()
        shard(b, 3, sibling).start()

    def expert(pair):
        x = held[pl.ds(2 * pair, 2)].reshape(2 * rows, features)

        @pl.loop(0, width // 256)
        def _(i):
            cols = pl.ds(pl.multiple_of(i * 256, 256), 256)
            g = jnp.dot(x, gate_v[:, cols], preferred_element_type=jnp.float32)
            u = jnp.dot(x, up_v[:, cols], preferred_element_type=jnp.float32)
            hidden[:, cols] = (g / (1.0 + jnp.exp(-g)) * u).astype(jnp.bfloat16)

        eye = lax.broadcasted_iota(jnp.int32, (rows, rows), 0) == lax.broadcasted_iota(
            jnp.int32, (rows, rows), 1
        )
        scale = jnp.concatenate(
            [
                jnp.sum(jnp.where(eye, factors[2 * pair + s][0:1, :], 0.0), axis=1, keepdims=True)
                for s in range(2)
            ],
            axis=0,
        )

        @pl.loop(0, features // 512)
        def _(i):
            cols = pl.ds(pl.multiple_of(i * 512, 512), 512)
            o = jnp.dot(hidden[...], down_v[:, cols], preferred_element_type=jnp.float32)
            o = (o * scale).astype(jnp.bfloat16)
            part[pl.ds(2 * pair, 2), :, cols] = o.reshape(2, rows, 512)

    def add(b, term, h):
        size = rows // CHUNKS

        @pl.loop(0, size // 16)
        def _(i):
            r = pl.ds(pl.multiple_of(h * size + i * 16, 16), 16)
            total = part[b, r, :].astype(jnp.float32) + term[r, :].astype(jnp.float32)
            part[b, r, :] = total.astype(jnp.bfloat16)

    def reduce_pairs(k):
        zo = order(k)
        for yo in (1 - y, y):
            pair = 2 * zo + yo
            half(pair, c).wait_recv()
            for h in range(CHUNKS):
                add(2 * pair + c, from_core.at[pair], h)
                if yo is not y:
                    cross(zo, h).start()

    @pl.loop(1, n)
    def _(i):
        weight((me + i) % n, me).start()

    mine = pltpu.make_async_copy(table.at[me], factors.at[me], f_send.at[me])
    mine.start()
    own.wait()
    forward(0)
    mine.wait()
    for load in loads:
        load.wait()

    @pl.loop(1, n)
    def _(i):
        weight(me, (me + i) % n).wait_recv()

    @pl.loop(0, depth)
    def _(k):
        zo = order(k)
        shard(zo * 4 + y * 2 + 1 - c, 3, sibling).wait_recv()
        expert(2 * zo + y)
        half(2 * zo + y, 1 - c).start()

        @pl.when(k < depth - 1)
        def _():
            forward(k + 1)

        if depth > 3:

            @pl.when(k == depth - 1)
            def _():
                reduce_pairs(1)

        b = zo * 4 + (1 - y) * 2 + c
        shard(b, 2, across).wait_recv()
        shard(b, 3, sibling).start()
        shard(b + 1 - 2 * c, 3, sibling).wait_recv()
        expert(2 * zo + 1 - y)
        half(2 * zo + 1 - y, 1 - c).start()

    last = [k for k in reversed(range(depth)) if depth < 4 or k != 1]

    @pl.loop(0, len(last))
    def _(i):
        reduce_pairs(jnp.where(i == len(last) - 1, 0, depth - 1 - i))

    @pl.loop(0, depth)
    def _(i):
        ends = jnp.where(i == depth - 1, 0, jnp.where(i == 0, 1, depth - i))
        zo = order(jnp.where((z == 0) | (z == depth - 1), ends, depth - 1 - i))
        b = zo * 4 + y * 2 + c

        @pl.loop(0, CHUNKS)
        def _(h):
            cross(zo, h).wait_recv()
            add(b, from_y.at[zo], h)

            @pl.when((zo >= z) & (z > 0))
            def _():
                along(zo, 0, h, me).wait_recv()
                add(b, from_z.at[0, zo], h)

            @pl.when((zo <= z) & (z < depth - 1))
            def _():
                along(zo, 1, h, me).wait_recv()
                add(b, from_z.at[1, zo], h)

            @pl.when(zo > z)
            def _():
                along(zo, 0, h, me + 4).start()

            @pl.when(zo < z)
            def _():
                along(zo, 1, h, me - 4).start()

    done = pltpu.make_async_copy(part.at[me], out, out_sem)
    done.start()

    @pl.loop(1, n)
    def _(i):
        weight((me + i) % n, me).wait_send()

    @pl.loop(0, depth)
    def _(zo):
        b = zo * 4 + y * 2 + c

        @pl.when((zo <= z) & (z < depth - 1))
        def _():
            shard(b, 0, me + 4).wait_send()

        @pl.when((zo >= z) & (z > 0))
        def _():
            shard(b, 1, me - 4).wait_send()

        shard(b, 2, across).wait_send()
        shard(b, 3, sibling).wait_send()
        shard(zo * 4 + (1 - y) * 2 + c, 3, sibling).wait_send()
        half(2 * zo, 1 - c).wait_send()
        half(2 * zo + 1, 1 - c).wait_send()
        for h in range(CHUNKS):
            cross(zo, h).wait_send()

        @pl.when(zo > z)
        def _():
            for h in range(CHUNKS):
                along(zo, 0, h, me + 4).wait_send()

        @pl.when(zo < z)
        def _():
            for h in range(CHUNKS):
                along(zo, 1, h, me - 4).wait_send()

    done.wait()


def exchange(n, tokens, table, w_gate, w_up, w_down):
    rows, features = tokens.shape
    width = w_gate.shape[1]
    depth = n // 4
    bf, dma = jnp.bfloat16, pltpu.SemaphoreType.DMA
    return pl.pallas_call(
        functools.partial(kernel, n),
        out_shape=jax.ShapeDtypeStruct((rows, features), bf),
        in_specs=[
            pl.BlockSpec(memory_space=pl.ANY),
            pl.BlockSpec(memory_space=pltpu.VMEM),
            pl.BlockSpec(memory_space=pl.ANY),
            pl.BlockSpec(memory_space=pl.ANY),
            pl.BlockSpec(memory_space=pl.ANY),
        ],
        out_specs=pl.BlockSpec(memory_space=pl.ANY),
        scratch_shapes=[
            pltpu.VMEM((n, rows, features), bf),
            pltpu.VMEM((n, 8, rows), jnp.float32),
            pltpu.VMEM((n, rows, features), bf),
            pltpu.VMEM((n // 2, rows, features), bf),
            pltpu.VMEM((depth, rows, features), bf),
            pltpu.VMEM((2, depth, rows, features), bf),
            pltpu.VMEM((features, width), bf),
            pltpu.VMEM((features, width), bf),
            pltpu.VMEM((width, features), bf),
            pltpu.VMEM((2 * rows, width), bf),
            dma, dma((3,)), dma((n,)), dma((n,)), dma((4, n)), dma((n,)),
            dma((n // 2,)), dma((n // 2,)), dma((depth, CHUNKS)), dma((depth, CHUNKS)),
            dma((depth, CHUNKS)), dma((2, depth, CHUNKS)), dma,
        ],
        compiler_params=pltpu.CompilerParams(
            collective_id=0, has_side_effects=True, vmem_limit_bytes=56 * 1024 * 1024
        ),
        cost_estimate=pl.CostEstimate(
            flops=6 * n * rows * features * width,
            bytes_accessed=6 * features * width + 4 * rows * features,
            transcendentals=n * rows * width,
        ),
    )(tokens, table, w_gate, w_up, w_down)


def collectives(tokens, routes, gate_weights, w_gate, w_up, w_down):
    rank = lax.axis_index("rank")
    everyone = lax.all_gather(tokens, "rank", axis=0, tiled=True)
    all_routes = lax.all_gather(routes, "rank", axis=0, tiled=True)
    all_gates = lax.all_gather(gate_weights, "rank", axis=0, tiled=True)
    factor = jnp.sum(jnp.where(all_routes == rank, all_gates, 0.0), axis=1)
    gate_proj = jnp.dot(everyone, w_gate, preferred_element_type=jnp.float32)
    up_proj = jnp.dot(everyone, w_up, preferred_element_type=jnp.float32)
    hidden = (jax.nn.silu(gate_proj) * up_proj).astype(jnp.bfloat16)
    expert_out = jnp.dot(hidden, w_down, preferred_element_type=jnp.float32)
    weighed = (factor[:, None] * expert_out).astype(jnp.bfloat16)
    return lax.psum_scatter(weighed, "rank", scatter_dimension=0, tiled=True)


def per_device(tokens, routes, gate_weights, token_order, w_gate, w_up, w_down):
    n = lax.axis_size("rank")
    rows, features = tokens.shape
    blocks, block_rows = token_order.shape
    own_weights = (w_gate[0], w_up[0], w_down[0])

    if n % 4 == 0 and n <= 16 and n * rows * features <= 4 * 1024 * 1024:
        chosen = routes.T[None] == jnp.arange(n, dtype=jnp.int32)[:, None, None]
        table = jnp.sum(jnp.where(chosen, gate_weights.T[None], 0.0), axis=1)
        table = jnp.broadcast_to(table[:, None, :], (n, 8, rows))
        combined = exchange(n, tokens, table, *own_weights)
    else:
        combined = collectives(tokens, routes, gate_weights, *own_weights)

    order = token_order + jnp.arange(blocks, dtype=jnp.int32)[:, None] * block_rows
    pick = (order.reshape(-1)[:, None] == jnp.arange(rows, dtype=jnp.int32)[None, :])
    return jnp.dot(
        pick.astype(jnp.bfloat16), combined, preferred_element_type=jnp.float32
    ).astype(jnp.bfloat16)


def solution(mesh):
    return jax.shard_map(
        per_device,
        mesh=mesh,
        in_specs=(
            P(("rep", "rank"), None),
            P(("rep", "rank"), None),
            P(("rep", "rank"), None),
            P(("rep", "rank"), None),
            P("rank", None, None),
            P("rank", None, None),
            P("rank", None, None),
        ),
        out_specs=P(("rep", "rank"), None),
        check_vma=False,
    )
```

```python
import functools

import jax
import jax.numpy as jnp
from jax import lax
from jax.experimental import pallas as pl
from jax.experimental.pallas import tpu as pltpu
from jax.sharding import PartitionSpec as P

MESH = pl.DeviceIdType.MESH
CHUNKS = 4


def kernel(
    n, tokens, table, w_gate, w_up, w_down, out,
    held, factors, part, from_core, from_y, from_z, gate_v, up_v, down_v, hidden,
    own_sem, w_sem, f_send, f_recv, ag_send, ag_recv,
    core_send, core_recv, y_send, y_recv, z_send, z_recv, out_sem,
):
    depth = n // 4
    rows, features = tokens.shape
    width = gate_v.shape[1]
    me = lax.axis_index("rank")
    z, y, c = me // 4, (me // 2) % 2, me % 2
    sibling = me + 1 - 2 * c
    across = me + 2 - 4 * y

    own = pltpu.make_async_copy(tokens, held.at[me], own_sem)
    own.start()
    loads = [
        pltpu.make_async_copy(a, b, w_sem.at[i])
        for i, (a, b) in enumerate(((w_gate, gate_v), (w_up, up_v), (w_down, down_v)))
    ]
    for load in loads:
        load.start()

    barrier = pltpu.get_barrier_semaphore()

    @pl.loop(1, n)
    def _(i):
        pl.semaphore_signal(barrier, inc=1, device_id={"rank": (me + i) % n}, device_id_type=MESH)

    pl.semaphore_wait(barrier, n - 1)

    def order(k):
        near = jnp.minimum(z, depth - 1 - z)
        step = (k + 1) // 2
        low = z <= depth - 1 - z
        both = jnp.where((k % 2 == 1) == low, z + step, z - step)
        one = jnp.where(low, k, depth - 1 - k)
        return jnp.where(k <= 2 * near, both, one)

    def remote(source, target, send, recv, to):
        return pltpu.make_async_remote_copy(
            src_ref=source, dst_ref=target, send_sem=send, recv_sem=recv,
            device_id={"rank": to}, device_id_type=MESH,
        )

    def shard(b, way, to):
        return remote(held.at[b], held.at[b], ag_send.at[way, b], ag_recv.at[b], to)

    def weight(to, source):
        return remote(table.at[to], factors.at[source], f_send.at[to], f_recv.at[source], to)

    def half(pair, side):
        b = 2 * pair + side
        return remote(part.at[b], from_core.at[pair], core_send.at[pair], core_recv.at[pair], sibling)

    def chunk(h):
        return pl.ds(h * (rows // CHUNKS), rows // CHUNKS)

    def cross(zo, h):
        return remote(
            part.at[zo * 4 + (1 - y) * 2 + c, chunk(h)], from_y.at[zo, chunk(h)],
            y_send.at[zo, h], y_recv.at[zo, h], across,
        )

    def along(zo, way, h, to):
        return remote(
            part.at[zo * 4 + y * 2 + c, chunk(h)], from_z.at[way, zo, chunk(h)],
            z_send.at[zo, h], z_recv.at[way, zo, h], to,
        )

    def forward(k):
        zo = order(k)
        b = zo * 4 + y * 2 + c

        @pl.when(zo != z)
        def _():
            shard(b, 0, me).wait_recv()

        @pl.when((zo <= z) & (z < depth - 1))
        def _():
            shard(b, 0, me + 4).start()

        @pl.when((zo >= z) & (z > 0))
        def _():
            shard(b, 1, me - 4).start()

        shard(b, 2, across).start()
        shard(b, 3, sibling).start()

    def expert(pair):
        x = held[pl.ds(2 * pair, 2)].reshape(2 * rows, features)

        @pl.loop(0, width // 256)
        def _(i):
            cols = pl.ds(pl.multiple_of(i * 256, 256), 256)
            g = jnp.dot(x, gate_v[:, cols], preferred_element_type=jnp.float32)
            u = jnp.dot(x, up_v[:, cols], preferred_element_type=jnp.float32)
            hidden[:, cols] = (g / (1.0 + jnp.exp(-g)) * u).astype(jnp.bfloat16)

        eye = lax.broadcasted_iota(jnp.int32, (rows, rows), 0) == lax.broadcasted_iota(
            jnp.int32, (rows, rows), 1
        )
        scale = jnp.concatenate(
            [
                jnp.sum(jnp.where(eye, factors[2 * pair + s][0:1, :], 0.0), axis=1, keepdims=True)
                for s in range(2)
            ],
            axis=0,
        )

        @pl.loop(0, features // 512)
        def _(i):
            cols = pl.ds(pl.multiple_of(i * 512, 512), 512)
            o = jnp.dot(hidden[...], down_v[:, cols], preferred_element_type=jnp.float32)
            o = (o * scale).astype(jnp.bfloat16)
            part[pl.ds(2 * pair, 2), :, cols] = o.reshape(2, rows, 512)

    def add(b, term, h):
        size = rows // CHUNKS

        @pl.loop(0, size // 16)
        def _(i):
            r = pl.ds(pl.multiple_of(h * size + i * 16, 16), 16)
            total = part[b, r, :].astype(jnp.float32) + term[r, :].astype(jnp.float32)
            part[b, r, :] = total.astype(jnp.bfloat16)

    def reduce_pairs(k):
        zo = order(k)
        for yo in (1 - y, y):
            pair = 2 * zo + yo
            half(pair, c).wait_recv()
            for h in range(CHUNKS):
                add(2 * pair + c, from_core.at[pair], h)
                if yo is not y:
                    cross(zo, h).start()

    own.wait()
    forward(0)

    @pl.loop(1, n)
    def _(i):
        weight((me + i) % n, me).start()

    mine = pltpu.make_async_copy(table.at[me], factors.at[me], f_send.at[me])
    mine.start()
    mine.wait()
    for load in loads:
        load.wait()

    @pl.loop(1, n)
    def _(i):
        weight(me, (me + i) % n).wait_recv()

    @pl.loop(0, depth)
    def _(k):
        zo = order(k)
        shard(zo * 4 + y * 2 + 1 - c, 3, sibling).wait_recv()
        expert(2 * zo + y)
        half(2 * zo + y, 1 - c).start()

        @pl.when(k < depth - 1)
        def _():
            forward(k + 1)

        if depth > 3:

            @pl.when(k == depth - 1)
            def _():
                reduce_pairs(1)

        b = zo * 4 + (1 - y) * 2 + c
        shard(b, 2, across).wait_recv()
        shard(b, 3, sibling).start()
        shard(b + 1 - 2 * c, 3, sibling).wait_recv()
        expert(2 * zo + 1 - y)
        half(2 * zo + 1 - y, 1 - c).start()

    last = [k for k in reversed(range(depth)) if depth < 4 or k != 1]

    @pl.loop(0, len(last))
    def _(i):
        reduce_pairs(jnp.where(i == len(last) - 1, 0, depth - 1 - i))

    @pl.loop(0, depth)
    def _(i):
        ends = jnp.where(i == depth - 1, 0, jnp.where(i == 0, 1, depth - i))
        zo = order(jnp.where((z == 0) | (z == depth - 1), ends, depth - 1 - i))
        b = zo * 4 + y * 2 + c

        @pl.loop(0, CHUNKS)
        def _(h):
            cross(zo, h).wait_recv()
            add(b, from_y.at[zo], h)

            @pl.when((zo >= z) & (z > 0))
            def _():
                along(zo, 0, h, me).wait_recv()
                add(b, from_z.at[0, zo], h)

            @pl.when((zo <= z) & (z < depth - 1))
            def _():
                along(zo, 1, h, me).wait_recv()
                add(b, from_z.at[1, zo], h)

            @pl.when(zo > z)
            def _():
                along(zo, 0, h, me + 4).start()

            @pl.when(zo < z)
            def _():
                along(zo, 1, h, me - 4).start()

    done = pltpu.make_async_copy(part.at[me], out, out_sem)
    done.start()

    @pl.loop(1, n)
    def _(i):
        weight((me + i) % n, me).wait_send()

    @pl.loop(0, depth)
    def _(zo):
        b = zo * 4 + y * 2 + c

        @pl.when((zo <= z) & (z < depth - 1))
        def _():
            shard(b, 0, me + 4).wait_send()

        @pl.when((zo >= z) & (z > 0))
        def _():
            shard(b, 1, me - 4).wait_send()

        shard(b, 2, across).wait_send()
        shard(b, 3, sibling).wait_send()
        shard(zo * 4 + (1 - y) * 2 + c, 3, sibling).wait_send()
        half(2 * zo, 1 - c).wait_send()
        half(2 * zo + 1, 1 - c).wait_send()
        for h in range(CHUNKS):
            cross(zo, h).wait_send()

        @pl.when(zo > z)
        def _():
            for h in range(CHUNKS):
                along(zo, 0, h, me + 4).wait_send()

        @pl.when(zo < z)
        def _():
            for h in range(CHUNKS):
                along(zo, 1, h, me - 4).wait_send()

    done.wait()


def exchange(n, tokens, table, w_gate, w_up, w_down):
    rows, features = tokens.shape
    width = w_gate.shape[1]
    depth = n // 4
    bf, dma = jnp.bfloat16, pltpu.SemaphoreType.DMA
    return pl.pallas_call(
        functools.partial(kernel, n),
        out_shape=jax.ShapeDtypeStruct((rows, features), bf),
        in_specs=[
            pl.BlockSpec(memory_space=pl.ANY),
            pl.BlockSpec(memory_space=pltpu.VMEM),
            pl.BlockSpec(memory_space=pl.ANY),
            pl.BlockSpec(memory_space=pl.ANY),
            pl.BlockSpec(memory_space=pl.ANY),
        ],
        out_specs=pl.BlockSpec(memory_space=pl.ANY),
        scratch_shapes=[
            pltpu.VMEM((n, rows, features), bf),
            pltpu.VMEM((n, 8, rows), jnp.float32),
            pltpu.VMEM((n, rows, features), bf),
            pltpu.VMEM((n // 2, rows, features), bf),
            pltpu.VMEM((depth, rows, features), bf),
            pltpu.VMEM((2, depth, rows, features), bf),
            pltpu.VMEM((features, width), bf),
            pltpu.VMEM((features, width), bf),
            pltpu.VMEM((width, features), bf),
            pltpu.VMEM((2 * rows, width), bf),
            dma, dma((3,)), dma((n,)), dma((n,)), dma((4, n)), dma((n,)),
            dma((n // 2,)), dma((n // 2,)), dma((depth, CHUNKS)), dma((depth, CHUNKS)),
            dma((depth, CHUNKS)), dma((2, depth, CHUNKS)), dma,
        ],
        compiler_params=pltpu.CompilerParams(
            collective_id=0, has_side_effects=True, vmem_limit_bytes=56 * 1024 * 1024
        ),
        cost_estimate=pl.CostEstimate(
            flops=6 * n * rows * features * width,
            bytes_accessed=6 * features * width + 4 * rows * features,
            transcendentals=n * rows * width,
        ),
    )(tokens, table, w_gate, w_up, w_down)


def collectives(tokens, routes, gate_weights, w_gate, w_up, w_down):
    rank = lax.axis_index("rank")
    everyone = lax.all_gather(tokens, "rank", axis=0, tiled=True)
    all_routes = lax.all_gather(routes, "rank", axis=0, tiled=True)
    all_gates = lax.all_gather(gate_weights, "rank", axis=0, tiled=True)
    factor = jnp.sum(jnp.where(all_routes == rank, all_gates, 0.0), axis=1)
    gate_proj = jnp.dot(everyone, w_gate, preferred_element_type=jnp.float32)
    up_proj = jnp.dot(everyone, w_up, preferred_element_type=jnp.float32)
    hidden = (jax.nn.silu(gate_proj) * up_proj).astype(jnp.bfloat16)
    expert_out = jnp.dot(hidden, w_down, preferred_element_type=jnp.float32)
    weighed = (factor[:, None] * expert_out).astype(jnp.bfloat16)
    return lax.psum_scatter(weighed, "rank", scatter_dimension=0, tiled=True)


def per_device(tokens, routes, gate_weights, token_order, w_gate, w_up, w_down):
    n = lax.axis_size("rank")
    rows, features = tokens.shape
    blocks, block_rows = token_order.shape
    own_weights = (w_gate[0], w_up[0], w_down[0])

    if n % 4 == 0 and n <= 16 and n * rows * features <= 4 * 1024 * 1024:
        chosen = routes.T[None] == jnp.arange(n, dtype=jnp.int32)[:, None, None]
        table = jnp.sum(jnp.where(chosen, gate_weights.T[None], 0.0), axis=1)
        table = jnp.broadcast_to(table[:, None, :], (n, 8, rows))
        combined = exchange(n, tokens, table, *own_weights)
    else:
        combined = collectives(tokens, routes, gate_weights, *own_weights)

    order = token_order + jnp.arange(blocks, dtype=jnp.int32)[:, None] * block_rows
    pick = (order.reshape(-1)[:, None] == jnp.arange(rows, dtype=jnp.int32)[None, :])
    return jnp.dot(
        pick.astype(jnp.bfloat16), combined, preferred_element_type=jnp.float32
    ).astype(jnp.bfloat16)


def solution(mesh):
    return jax.shard_map(
        per_device,
        mesh=mesh,
        in_specs=(
            P(("rep", "rank"), None),
            P(("rep", "rank"), None),
            P(("rep", "rank"), None),
            P(("rep", "rank"), None),
            P("rank", None, None),
            P("rank", None, None),
            P("rank", None, None),
        ),
        out_specs=P(("rep", "rank"), None),
        check_vma=False,
    )
```
